256 devices in a mesh: grp: 16 (over x, y), col: 16 (over z, core).
Axes of the slice: x: 4, y: 4, z: 8, core: 2. Of those that a mesh axis runs over, the one named last changes fastest.
Arguments:
- features: bfloat16 [128, 1048576], P('col', 'grp'), may hold values from -6 to 6
- adj_tiles: bfloat16 [4096, 128, 128], P('grp'), may hold values from -0.125 to 0.125
- tile_dst: int32 [4096], P('grp'), may hold values from 0 to 15
- tile_src: int32 [4096], P('grp'), may hold values from 0 to 8191, as said below
- dst_ids: int32 [256], P('grp'), may hold values from 0 to 8191, as said below
- self_coef: float32 [32768], P('grp'), may hold values from 0.2 to 2
- weight: bfloat16 [128, 128], replicated, may hold values from -0.5 to 0.5
- out_bias: float32 [128], replicated, may hold values from -3 to 3
Outputs:
- layer_out: bfloat16 [32768, 128], P(('grp', 'col'))
The draws below stay inside these ranges and needn't reach their ends.
Inputs may be any that keep to these rules, and one draw needn't show every extreme that they name: `tile_src`: tiles of group k name, of every other group, exactly 4 distinct source blocks; the rest name blocks of group k. `dst_ids`: the destination blocks of group k are distinct blocks stored in group k.
All inputs are finite; a program needn't handle non-finite values.
Results may differ from the reference program's by a relative error of at most 0.0047.
Values may be sent and summed in bfloat16 or wider, within the bound.
No kernel may reach another device: no remote copies, remote signals or barrier semaphores. Data moves between devices by JAX's collectives and lax.ppermute only.
A program may use at most 64 MiB of HBM per device.

```python
import math
import jax
import jax.numpy as jnp
from jax import lax

F = 128
FO = 128
BLOCK = 128
BLK_DEV = 32
DST_DEV = 1
TILES_GRP = 256
NEED = 4
SRC_BLOCKS = 8192
DST_GRP = 16
DST_BLOCKS = 256
TILES = 4096
N_GRP = 16
N_COL = 16


def draw_tile_src(key, part):
    key = jax.random.fold_in(key, 11)
    group_keys = jax.random.split(key, N_GRP)
    group_len = BLK_DEV * N_COL
    remote_count = (N_GRP - 1) * NEED
    spare_count = TILES_GRP - remote_count

    def draw_group(group_id, group_key):
        subkeys = jax.random.split(group_key, 5)
        set_keys = jax.random.split(subkeys[0], N_GRP)
        chosen_sets = jax.vmap(lambda inner: jax.random.permutation(inner, group_len)[:NEED])(set_keys)
        others = (group_id + 1 + jnp.arange(N_GRP - 1, dtype=jnp.int32)) % N_GRP
        needed = (others[:, None] * group_len + chosen_sets[others]).reshape(-1)
        remote_ids = needed[jax.random.randint(subkeys[1], (spare_count,), 0, remote_count)]
        local_ids = group_id * group_len + jax.random.randint(subkeys[2], (spare_count,), 0, group_len)
        coin_flips = jax.random.randint(subkeys[3], (spare_count,), 0, 2)
        listed = jnp.concatenate([needed, jnp.where(coin_flips == 0, local_ids, remote_ids)])
        return listed[jax.random.permutation(subkeys[4], TILES_GRP)]
    result = jax.vmap(draw_group)(jnp.arange(N_GRP, dtype=jnp.int32), group_keys)
    return result.reshape(-1).astype(jnp.int32)


def draw_dst_ids(key, part):
    key = jax.random.fold_in(key, 12)
    group_keys = jax.random.split(key, N_GRP)
    group_len = BLK_DEV * N_COL

    def draw_group(group_id, group_key):
        return group_id * group_len + jax.random.permutation(group_key, group_len)[:DST_DEV * N_COL]
    result = jax.vmap(draw_group)(jnp.arange(N_GRP, dtype=jnp.int32), group_keys)
    return result.reshape(-1).astype(jnp.int32)


def place_ends(array, stream_key, least, largest):
    longest = array.shape.index(max(array.shape))
    spots = []
    for shift in (0, 1):
        where = [jax.random.randint(jax.random.fold_in(stream_key, axis), (), 0, length) for axis, length in enumerate(array.shape)]
        where[longest] = (where[longest] + shift) % array.shape[longest]
        spots.append(tuple(where))
    return array.at[spots[0]].set(least).at[spots[1]].set(largest)


def steps_of(stream_key, dims, shards, least, high):
    factor_of = 1.0
    for axis_at, shards_of in shards:
        heights = jax.random.uniform(jax.random.fold_in(jax.random.fold_in(stream_key, 6), axis_at), (shards_of,), jnp.float32, least / len(shards), high / len(shards))
        factor_of = factor_of * jnp.repeat(jnp.exp(heights), dims[axis_at] // shards_of).reshape((-1,) + (1,) * (len(dims) - 1 - axis_at))
    return factor_of


def noise(rng, shape, deviation, most, cuts=(), held_as=jnp.bfloat16):
    entries = jax.random.normal(rng, shape, jnp.float32) * deviation
    if len(cuts) > 0:
        entries = steps_of(rng, shape, cuts, -0.22, 0.18) * entries
    return jnp.clip(entries, min=-most, max=most).astype(held_as)


def setup_inputs(seed: int = 0) -> dict:
    key_of = jax.random.split(jax.random.key(seed), 9)
    features = noise(key_of[0], (F, SRC_BLOCKS * BLOCK), 1.0, 6.0, ((0, 16), (1, 16)))
    adj_tiles = noise(key_of[1], (TILES, BLOCK, BLOCK), (BLOCK * TILES_GRP // (DST_DEV * N_COL)) ** -0.5, 0.125, ((0, 16),))
    tile_dst = place_ends(jax.random.randint(key_of[2], (TILES,), 0, DST_DEV * N_COL), jax.random.fold_in(key_of[2], 1), 0, (DST_DEV * N_COL) - 1).astype(jnp.int32)
    tile_src = draw_tile_src(jax.random.fold_in(key_of[8], 71), 0)
    dst_ids = draw_dst_ids(jax.random.fold_in(key_of[8], 71), 0)
    self_coef = jnp.clip(jnp.exp(math.log(2.0) - 2.3025851 * jax.random.uniform(key_of[5], (DST_BLOCKS * BLOCK,), jnp.float32) ** steps_of(key_of[5], (DST_BLOCKS * BLOCK,), ((0, 16),), -0.2, 0.2)), 0.2, 2.0)
    weight = noise(key_of[6], (F, FO), F ** -0.5, 0.5)
    out_bias = noise(key_of[7], (FO,), 0.5, 3.0, (), jnp.float32)
    return {"features": features, "adj_tiles": adj_tiles, "tile_dst": tile_dst, "tile_src": tile_src, "dst_ids": dst_ids, "self_coef": self_coef, "weight": weight, "out_bias": out_bias}


def reference(features, adj_tiles, tile_dst, tile_src, dst_ids, self_coef, weight, out_bias):
    blocks = features.reshape(F, SRC_BLOCKS, BLOCK)
    tiles_grouped = adj_tiles.reshape(N_GRP, TILES_GRP, BLOCK, BLOCK)

    def per_group(group_index):
        sources = lax.dynamic_slice_in_dim(tile_src, group_index * TILES_GRP, TILES_GRP)
        targets = lax.dynamic_slice_in_dim(tile_dst, group_index * TILES_GRP, TILES_GRP)
        picked = jnp.take(blocks, sources, axis=1).astype(jnp.float32)
        tile_set = tiles_grouped[group_index].astype(jnp.float32)
        products = jnp.einsum('ftj,tij->tfi', picked, tile_set)
        onehot = (targets[None, :] == jnp.arange(DST_GRP, dtype=jnp.int32)[:, None]).astype(jnp.float32)
        summed = jnp.einsum('dt,tfi->dfi', onehot, products, precision=lax.Precision.HIGHEST)
        own_ids = lax.dynamic_slice_in_dim(dst_ids, group_index * DST_GRP, DST_GRP)
        own_feats = jnp.take(blocks, own_ids, axis=1).astype(jnp.float32).transpose(1, 0, 2)
        coefs = lax.dynamic_slice_in_dim(self_coef, group_index * DST_GRP * BLOCK, DST_GRP * BLOCK)
        coefs = coefs.reshape(DST_GRP, 1, BLOCK)
        return (summed + coefs * own_feats).astype(jnp.bfloat16)

    grouped = lax.map(per_group, jnp.arange(N_GRP, dtype=jnp.int32))
    aggregated = grouped.transpose(0, 1, 3, 2).reshape(DST_BLOCKS * BLOCK, F)
    mixed = jnp.dot(aggregated, weight, preferred_element_type=jnp.float32) + out_bias
    return jax.nn.relu(mixed).astype(jnp.bfloat16)
```

```python
import jax
import jax.numpy as jnp
from jax import lax
from jax.experimental import pallas as pl
from jax.experimental.pallas import tpu as pltpu
from jax.sharding import PartitionSpec as P

NEED = 4
BATCH = 16
BIG = 1 << 30

VMEM = pl.BlockSpec(memory_space=pltpu.VMEM)
SMEM = pl.BlockSpec(memory_space=pltpu.SMEM)


def four_least(values):
    least = []
    for _ in range(NEED):
        low = jnp.min(values, axis=1, keepdims=True)
        least.append(low)
        values = jnp.where(values > low, values, BIG)
    return least


def tile_products(entries, count, load_x, adj_ref, acc_ref):
    zero = jnp.zeros((8, 128), jnp.float32)

    def one_pass(step, carry):
        results = []
        for quad in range(BATCH // 4):
            tiles, xs, dsts = [], [], []
            for q in range(4):
                entry = entries[step * BATCH + quad * 4 + q]
                tiles.append(adj_ref[entry & 255])
                xs.append(load_x(entry >> 13))
                dsts.append((entry >> 8) & 31)
            left = jnp.concatenate([xs[0], zero, xs[2], zero], axis=0)
            right = jnp.concatenate([zero, xs[1], zero, xs[3]], axis=0)
            lhs = jnp.concatenate([left, right], axis=1).astype(jnp.bfloat16)
            rhs = jnp.concatenate(
                [
                    jnp.concatenate([tiles[0], tiles[1]], axis=1),
                    jnp.concatenate([tiles[2], tiles[3]], axis=1),
                ],
                axis=0,
            )
            out = lax.dot_general(
                lhs, rhs, (((1,), (1,)), ((), ())), preferred_element_type=jnp.float32
            )
            results += [
                (dsts[0], out[0:8, 0:128]),
                (dsts[1], out[8:16, 0:128]),
                (dsts[2], out[16:24, 128:256]),
                (dsts[3], out[24:32, 128:256]),
            ]
        for dst, value in results:
            acc_ref[dst] += value
        return carry

    lax.fori_loop(0, (count + BATCH - 1) // BATCH, one_pass, 0)


def local_kernel(
    src_s, dst_s, ids_s, src_v, coef_ref, feat_ref, adj_ref,
    acc_ref, remote_s, counts_s,
    local_s, slot_v, slot_s, sem,
):
    n_tiles = src_s.shape[0]
    group = lax.axis_index("grp")
    group_len = feat_ref.shape[1] // 128
    n_dst = ids_s.shape[0]
    n_grp = lax.axis_size("grp")
    shift = group_len.bit_length() - 1
    src = jnp.broadcast_to(src_v[...], (n_grp, n_tiles))
    mine = (src >> shift) == lax.broadcasted_iota(jnp.int32, (n_grp, n_tiles), 0)
    least = four_least(jnp.where(mine, src, BIG))
    rank = jnp.zeros((n_grp, n_tiles), jnp.int32)
    for low in least[: NEED - 1]:
        rank += jnp.where(mine & (src > low), 1, 0)
    slot_v[...] = (src_v[...] >> shift) * NEED + jnp.sum(rank, axis=0, keepdims=True)
    copy = pltpu.make_async_copy(slot_v, slot_s, sem)
    copy.start()
    for d in range(n_dst):
        place = pl.multiple_of((ids_s[d] - group * group_len) * 128, 128)
        own = feat_ref[:, pl.ds(place, 128)].astype(jnp.float32)
        acc_ref[d] = coef_ref[d : d + 1, :] * own
    acc_ref[n_dst] = jnp.zeros((8, 128), jnp.float32)
    copy.wait()

    def sort_out(t, carry):
        n_local, n_remote = carry
        source = src_s[t]
        head = t + dst_s[t] * 256
        is_local = jnp.where((source >> shift) == group, 1, 0)
        local_s[n_local] = head + (source & (group_len - 1)) * 8192
        remote_s[n_remote] = head + slot_s[0, t] * 8192
        return n_local + is_local, n_remote + 1 - is_local

    n_local, n_remote = lax.fori_loop(0, n_tiles, sort_out, (0, 0), unroll=8)
    for i in range(BATCH):
        local_s[n_local + i] = n_dst * 256
        remote_s[n_remote + i] = n_dst * 256
    counts_s[0] = n_remote

    def load_x(place):
        return feat_ref[:, pl.ds(pl.multiple_of(place * 128, 128), 128)].astype(jnp.float32)

    tile_products(local_s, n_local, load_x, adj_ref, acc_ref)


def gather_kernel(req_ref, feat_ref, out_ref, place_v, place_s, sem):
    group = lax.axis_index("grp")
    group_len = feat_ref.shape[1] // 128
    shift = group_len.bit_length() - 1
    n_grp, n_tiles = req_ref.shape
    req = req_ref[...]
    least = four_least(jnp.where((req >> shift) == group, req & (group_len - 1), BIG))
    lane = lax.broadcasted_iota(jnp.int32, (n_grp, 128), 1)
    table = jnp.zeros((n_grp, 128), jnp.int32)
    for r, low in enumerate(least):
        table = jnp.where(lane == r, jnp.minimum(low, group_len - 1), table)
    place_v[...] = table
    copy = pltpu.make_async_copy(place_v, place_s, sem)
    copy.start()
    copy.wait()
    for k in range(n_grp):
        for r in range(NEED):
            place = pl.multiple_of(place_s[k, r] * 128, 128)
            out_ref[k, r] = feat_ref[:, pl.ds(place, 128)]


def remote_kernel(remote_s, counts_s, recv_ref, acc_in_ref, adj_ref, out_ref, acc_ref, x_ref):
    acc_ref[...] = acc_in_ref[...]
    x_ref[...] = recv_ref[...].astype(jnp.float32)

    def load_x(slot):
        return x_ref[slot]

    tile_products(remote_s, counts_s[0], load_x, adj_ref, acc_ref)
    out_ref[...] = acc_ref[: out_ref.shape[0]].astype(out_ref.dtype)


def per_device(features, adj_tiles, tile_dst, tile_src, dst_ids, self_coef, weight, out_bias):
    n_feat = features.shape[0]
    n_tiles = tile_src.shape[0]
    n_dst = dst_ids.shape[0]
    n_grp = lax.axis_size("grp")
    n_slots = n_grp * NEED
    params = pltpu.CompilerParams(vmem_limit_bytes=32 << 20)
    requests = lax.all_to_all(
        jnp.broadcast_to(tile_src, (n_grp, n_tiles)), "grp", 0, 0, tiled=True
    )
    acc, remote, counts = pl.pallas_call(
        local_kernel,
        name="local",
        out_shape=(
            jax.ShapeDtypeStruct((n_dst + 1, n_feat, 128), jnp.float32),
            jax.ShapeDtypeStruct((n_tiles + BATCH,), jnp.int32),
            jax.ShapeDtypeStruct((1,), jnp.int32),
        ),
        in_specs=[SMEM, SMEM, SMEM, VMEM, VMEM, VMEM, VMEM],
        out_specs=(VMEM, SMEM, SMEM),
        scratch_shapes=[
            pltpu.SMEM((n_tiles + BATCH,), jnp.int32),
            pltpu.VMEM((1, n_tiles), jnp.int32),
            pltpu.SMEM((1, n_tiles), jnp.int32),
            pltpu.SemaphoreType.DMA,
        ],
        compiler_params=params,
        cost_estimate=pl.CostEstimate(
            flops=2 * n_tiles * 128 * 128 * 32, bytes_accessed=9 << 20, transcendentals=0
        ),
    )(
        tile_src, tile_dst, dst_ids, tile_src.reshape(1, n_tiles),
        self_coef.reshape(n_dst, 128), features, adj_tiles,
    )
    blocks = pl.pallas_call(
        gather_kernel,
        name="gather",
        out_shape=jax.ShapeDtypeStruct((n_grp, NEED, n_feat, 128), features.dtype),
        in_specs=[VMEM, VMEM],
        out_specs=VMEM,
        scratch_shapes=[
            pltpu.VMEM((n_grp, 128), jnp.int32),
            pltpu.SMEM((n_grp, 128), jnp.int32),
            pltpu.SemaphoreType.DMA,
        ],
        compiler_params=params,
    )(requests, features)
    arrived = lax.all_to_all(blocks, "grp", 0, 0, tiled=True).reshape(n_slots, n_feat, 128)
    aggregated = pl.pallas_call(
        remote_kernel,
        name="remote",
        out_shape=jax.ShapeDtypeStruct((n_dst, n_feat, 128), jnp.bfloat16),
        in_specs=[SMEM, SMEM, VMEM, VMEM, VMEM],
        out_specs=VMEM,
        scratch_shapes=[
            pltpu.VMEM((n_dst + 1, n_feat, 128), jnp.float32),
            pltpu.VMEM((n_slots, n_feat, 128), jnp.float32),
        ],
        compiler_params=params,
    )(remote, counts, arrived, acc, adj_tiles)
    rows = lax.all_to_all(aggregated, "col", 0, 0, tiled=True).reshape(-1, 128)
    mixed = (
        lax.dot_general(
            rows, weight, (((0,), (0,)), ((), ())), preferred_element_type=jnp.float32
        )
        + out_bias
    )
    return jax.nn.relu(mixed).astype(jnp.bfloat16)


def solution(mesh):
    in_specs = (
        P("col", "grp"),
        P("grp", None, None),
        P("grp"),
        P("grp"),
        P("grp"),
        P("grp"),
        P(),
        P(),
    )
    out_specs = P(("grp", "col"), None)
    return jax.shard_map(
        per_device, mesh=mesh, in_specs=in_specs, out_specs=out_specs, check_vma=False
    )
```

```python
import jax
import jax.numpy as jnp
from jax import lax
from jax.experimental import pallas as pl
from jax.experimental.pallas import tpu as pltpu
from jax.sharding import PartitionSpec as P

NEED = 4
BATCH = 32
HELD = 64
CHUNK = 32
BIG = 1 << 30

VMEM = pl.BlockSpec(memory_space=pltpu.VMEM)
SMEM = pl.BlockSpec(memory_space=pltpu.SMEM)
HBM = pl.BlockSpec(memory_space=pltpu.HBM)


def four_least(values):
    least = []
    for _ in range(NEED):
        low = jnp.min(values, axis=1, keepdims=True)
        least.append(low)
        values = jnp.where(values > low, values, BIG)
    return least


def tile_products(entries, first, last, load_x, load_tile, acc_ref, before=None):
    zero = jnp.zeros((8, 128), jnp.float32)

    def one_pass(step, carry):
        if before is not None:
            carry = before(entries[step * BATCH + BATCH - 1] & 255, carry)
        results = []
        for pair in range(BATCH // 2):
            tiles, xs, dsts = [], [], []
            for q in range(2):
                entry = entries[step * BATCH + pair * 2 + q]
                tiles.append(load_tile(entry & 255))
                xs.append(load_x(entry >> 13))
                dsts.append((entry >> 8) & 31)
            left = jnp.concatenate([xs[0], zero], axis=0)
            right = jnp.concatenate([zero, xs[1]], axis=0)
            lhs = jnp.concatenate([left, right], axis=1).astype(jnp.bfloat16)
            rhs = jnp.concatenate(tiles, axis=1)
            out = lax.dot_general(
                lhs, rhs, (((1,), (1,)), ((), ())), preferred_element_type=jnp.float32
            )
            results += [(dsts[0], out[0:8]), (dsts[1], out[8:16])]
        for dst, value in results:
            acc_ref[dst] += value
        return carry

    return lax.fori_loop(first // BATCH, (last + BATCH - 1) // BATCH, one_pass, 0)


def local_kernel(
    src_h, src_row_h, dst_h, ids_h, coef_h, feat_h, adj_h,
    acc_ref, feat_ref, held_ref, remote_s,
    adj_ref, src_s, src_v, dst_s, ids_s, coef_ref, local_s, slot_v, slot_s, sems,
):
    copies = [
        pltpu.make_async_copy(a, b, sems.at[i])
        for i, (a, b) in enumerate(
            [
                (src_row_h, src_v), (src_h, src_s), (dst_h, dst_s), (ids_h, ids_s),
                (coef_h, coef_ref), (feat_h, feat_ref), (adj_h, adj_ref),
                (adj_h.at[pl.ds(0, HELD)], held_ref), (slot_v, slot_s),
            ]
        )
    ]
    for copy in copies[:-1]:
        copy.start()
    n_tiles = src_s.shape[0]
    group = lax.axis_index("grp")
    group_len = feat_ref.shape[1] // 128
    n_dst = ids_s.shape[0]
    n_grp = lax.axis_size("grp")
    shift = group_len.bit_length() - 1
    copies[0].wait()
    src = jnp.broadcast_to(src_v[...], (n_grp, n_tiles))
    mine = (src >> shift) == lax.broadcasted_iota(jnp.int32, (n_grp, n_tiles), 0)
    least = four_least(jnp.where(mine, src, BIG))
    rank = jnp.zeros((n_grp, n_tiles), jnp.int32)
    for low in least[: NEED - 1]:
        rank += jnp.where(mine & (src > low), 1, 0)
    slot_v[...] = (src_v[...] >> shift) * NEED + jnp.sum(rank, axis=0, keepdims=True)
    copies[-1].start()
    for copy in copies[1:5] + copies[-1:]:
        copy.wait()

    def sort_out(t, carry):
        n_local, n_remote = carry
        source = src_s[t]
        head = t + dst_s[t] * 256
        is_local = jnp.where((source >> shift) == group, 1, 0)
        local_s[n_local] = head + (source & (group_len - 1)) * 8192
        remote_s[n_remote] = head + slot_s[0, t] * 8192
        return n_local + is_local, n_remote + 1 - is_local

    n_local, n_early = lax.fori_loop(0, HELD, sort_out, (0, 0), unroll=8)
    for i in range(BATCH):
        remote_s[n_early + i] = n_dst * 256
    late = (n_early + BATCH - 1) // BATCH * BATCH
    n_local, n_late = lax.fori_loop(HELD, n_tiles, sort_out, (n_local, late), unroll=8)
    for i in range(BATCH):
        local_s[n_local + i] = n_dst * 256
        remote_s[n_late + i] = n_dst * 256 + n_tiles - 1
    remote_s[remote_s.shape[0] - 2] = late
    remote_s[remote_s.shape[0] - 1] = n_late
    copies[5].wait()
    for d in range(n_dst):
        place = pl.multiple_of((ids_s[d] - group * group_len) * 128, 128)
        own = feat_ref[:, pl.ds(place, 128)].astype(jnp.float32)
        acc_ref[d] = coef_ref[d : d + 1, :] * own
    acc_ref[n_dst] = jnp.zeros((8, 128), jnp.float32)
    copies[6].wait()

    def load_x(place):
        return feat_ref[:, pl.ds(pl.multiple_of(place * 128, 128), 128)].astype(jnp.float32)

    tile_products(local_s, 0, n_local, load_x, adj_ref.__getitem__, acc_ref)
    copies[7].wait()


def gather_kernel(req_ref, feat_ref, out_ref, place_v, place_s, sem):
    group = lax.axis_index("grp")
    group_len = feat_ref.shape[1] // 128
    shift = group_len.bit_length() - 1
    n_grp, n_tiles = req_ref.shape
    req = req_ref[...]
    least = four_least(jnp.where((req >> shift) == group, req & (group_len - 1), BIG))
    lane = lax.broadcasted_iota(jnp.int32, (n_grp, 128), 1)
    table = jnp.zeros((n_grp, 128), jnp.int32)
    for r, low in enumerate(least):
        table = jnp.where(lane == r, jnp.minimum(low, group_len - 1), table)
    place_v[...] = table
    copy = pltpu.make_async_copy(place_v, place_s, sem)
    copy.start()
    copy.wait()
    for k in range(n_grp):
        for r in range(NEED):
            place = pl.multiple_of(place_s[k, r] * 128, 128)
            out_ref[k, r] = feat_ref[:, pl.ds(place, 128)]


def remote_kernel(
    remote_s, recv_ref, acc_in_ref, held_ref, adj_h, out_ref, adj_ref, acc_ref, x_ref, sems
):
    n_tiles = adj_h.shape[0]
    n_chunks = (n_tiles - HELD) // CHUNK

    def chunk(i):
        first = pl.multiple_of(i * CHUNK, CHUNK)
        return pltpu.make_async_copy(
            adj_h.at[pl.ds(first + HELD, CHUNK)], adj_ref.at[pl.ds(first, CHUNK)], sems.at[i]
        )

    def start(i, carry):
        chunk(i).start()
        return carry

    def wait(i, carry):
        chunk(i).wait()
        return carry

    def arrived(tile, ready):
        needed = jnp.maximum(ready, (tile - HELD) // CHUNK + 1)
        lax.fori_loop(ready, needed, wait, 0)
        return needed

    lax.fori_loop(0, n_chunks, start, 0, unroll=True)
    acc_ref[...] = acc_in_ref[...]
    x_ref[...] = recv_ref[...].astype(jnp.float32)
    late = remote_s[remote_s.shape[0] - 2]
    tile_products(remote_s, 0, late, x_ref.__getitem__, held_ref.__getitem__, acc_ref)
    ready = tile_products(
        remote_s, late, remote_s[remote_s.shape[0] - 1], x_ref.__getitem__,
        lambda tile: adj_ref[tile - HELD], acc_ref, arrived,
    )
    lax.fori_loop(ready, n_chunks, wait, 0)
    out_ref[...] = acc_ref[: out_ref.shape[0]].astype(out_ref.dtype)


def per_device(features, adj_tiles, tile_dst, tile_src, dst_ids, self_coef, weight, out_bias):
    n_feat = features.shape[0]
    n_tiles = tile_src.shape[0]
    n_dst = dst_ids.shape[0]
    n_grp = lax.axis_size("grp")
    n_slots = n_grp * NEED
    params = pltpu.CompilerParams(vmem_limit_bytes=16 << 20)
    requests = lax.all_to_all(
        jnp.broadcast_to(tile_src, (n_grp, n_tiles)), "grp", 0, 0, tiled=True
    )
    acc, feat_held, adj_held, remote = pl.pallas_call(
        local_kernel,
        name="local",
        out_shape=(
            pltpu.VMEM((n_dst + 1, n_feat, 128), jnp.float32),
            pltpu.VMEM(features.shape, features.dtype),
            pltpu.VMEM((HELD,) + adj_tiles.shape[1:], adj_tiles.dtype),
            pltpu.SMEM((n_tiles + 2 * BATCH + 2,), jnp.int32),
        ),
        in_specs=[HBM] * 7,
        out_specs=(VMEM, VMEM, VMEM, SMEM),
        scratch_shapes=[
            pltpu.VMEM(adj_tiles.shape, adj_tiles.dtype),
            pltpu.SMEM((n_tiles,), jnp.int32),
            pltpu.VMEM((1, n_tiles), jnp.int32),
            pltpu.SMEM((n_tiles,), jnp.int32),
            pltpu.SMEM((n_dst,), jnp.int32),
            pltpu.VMEM((n_dst, 128), jnp.float32),
            pltpu.SMEM((n_tiles + BATCH,), jnp.int32),
            pltpu.VMEM((1, n_tiles), jnp.int32),
            pltpu.SMEM((1, n_tiles), jnp.int32),
            pltpu.SemaphoreType.DMA((9,)),
        ],
        compiler_params=params,
        cost_estimate=pl.CostEstimate(
            flops=2 * n_tiles * 128 * 128 * 32, bytes_accessed=18 << 20, transcendentals=0
        ),
    )(
        *[
            pltpu.with_memory_space_constraint(a, pltpu.HBM)
            for a in (
                tile_src, tile_src.reshape(1, n_tiles), tile_dst, dst_ids,
                self_coef.reshape(n_dst, 128), features, adj_tiles,
            )
        ]
    )
    blocks = pl.pallas_call(
        gather_kernel,
        name="gather",
        out_shape=jax.ShapeDtypeStruct((n_grp, NEED, n_feat, 128), features.dtype),
        in_specs=[VMEM, VMEM],
        out_specs=VMEM,
        scratch_shapes=[
            pltpu.VMEM((n_grp, 128), jnp.int32),
            pltpu.SMEM((n_grp, 128), jnp.int32),
            pltpu.SemaphoreType.DMA,
        ],
        compiler_params=params,
    )(requests, pltpu.with_memory_space_constraint(feat_held, pltpu.VMEM))
    arrived = lax.all_to_all(blocks, "grp", 0, 0, tiled=True).reshape(n_slots, n_feat, 128)
    aggregated = pl.pallas_call(
        remote_kernel,
        name="remote",
        out_shape=jax.ShapeDtypeStruct((n_dst, n_feat, 128), jnp.bfloat16),
        in_specs=[SMEM, VMEM, VMEM, VMEM, HBM],
        out_specs=VMEM,
        scratch_shapes=[
            pltpu.VMEM((n_tiles - HELD,) + adj_tiles.shape[1:], adj_tiles.dtype),
            pltpu.VMEM((n_dst + 1, n_feat, 128), jnp.float32),
            pltpu.VMEM((n_slots, n_feat, 128), jnp.float32),
            pltpu.SemaphoreType.DMA(((n_tiles - HELD) // CHUNK,)),
        ],
        compiler_params=params,
    )(
        remote, arrived, pltpu.with_memory_space_constraint(acc, pltpu.VMEM),
        pltpu.with_memory_space_constraint(adj_held, pltpu.VMEM),
        pltpu.with_memory_space_constraint(adj_tiles, pltpu.HBM),
    )
    rows = lax.all_to_all(aggregated, "col", 0, 0, tiled=True).reshape(-1, 128)
    mixed = (
        lax.dot_general(
            rows, weight, (((0,), (0,)), ((), ())), preferred_element_type=jnp.float32
        )
        + out_bias
    )
    return jax.nn.relu(mixed).astype(jnp.bfloat16)


def solution(mesh):
    in_specs = (
        P("col", "grp"),
        P("grp", None, None),
        P("grp"),
        P("grp"),
        P("grp"),
        P("grp"),
        P(),
        P(),
    )
    out_specs = P(("grp", "col"), None)
    return jax.shard_map(
        per_device, mesh=mesh, in_specs=in_specs, out_specs=out_specs, check_vma=False
    )
```

```python
import jax
import jax.numpy as jnp
from jax import lax
from jax.experimental import pallas as pl
from jax.experimental.pallas import tpu as pltpu
from jax.sharding import PartitionSpec as P

NEED = 4
BATCH = 32
HELD = 96
FETCH = 8
PAD = 40
CHUNK = 16
EARLY = 2
BIG = 1 << 30
LOCAL_BIT = 24
LOCAL = 1 << LOCAL_BIT

VMEM = pl.BlockSpec(memory_space=pltpu.VMEM)
SMEM = pl.BlockSpec(memory_space=pltpu.SMEM)
HBM = pl.BlockSpec(memory_space=pltpu.HBM)


def four_least(values):
    least = []
    for _ in range(NEED):
        low = jnp.min(values, axis=1, keepdims=True)
        least.append(low)
        values = jnp.where(values > low, values, BIG)
    return least


def tile_pass(entries, first, count, load_x, load_tile, acc_ref):
    zero = jnp.zeros((8, 128), jnp.float32)
    results = []
    for pair in range(count // 2):
        tiles, xs, dsts = [], [], []
        for q in range(2):
            index = first + pair * 2 + q
            entry = entries[index]
            tiles.append(load_tile(index, entry & 255))
            xs.append(load_x((entry >> 13) & 2047))
            dsts.append((entry >> 8) & 31)
        left = jnp.concatenate([xs[0], zero], axis=0)
        right = jnp.concatenate([zero, xs[1]], axis=0)
        lhs = jnp.concatenate([left, right], axis=1).astype(jnp.bfloat16)
        rhs = jnp.concatenate(tiles, axis=1)
        out = lax.dot_general(
            lhs, rhs, (((1,), (1,)), ((), ())), preferred_element_type=jnp.float32
        )
        results += [(dsts[0], out[0:8]), (dsts[1], out[8:16])]
    for dst, value in results:
        acc_ref[dst] += value


def tile_passes(entries, first, last, load_x, load_tile, acc_ref, wait_until, ready):
    def one_pass(step, ready):
        ready = wait_until(entries[step * BATCH + BATCH - 1] & 255, ready)
        tile_pass(entries, step * BATCH, BATCH, load_x, load_tile, acc_ref)
        return ready

    return lax.fori_loop(first, last, one_pass, ready)


def chunked_fetch(adj_h, adj_ref, sems):
    def chunk(i):
        tiles = pl.ds(pl.multiple_of(i * CHUNK, CHUNK), CHUNK)
        return pltpu.make_async_copy(adj_h.at[tiles], adj_ref.at[tiles], sems.at[i])

    def start(i, carry):
        chunk(i).start()
        return carry

    def wait(i, carry):
        chunk(i).wait()
        return carry

    def wait_until(tile, ready):
        needed = jnp.maximum(ready, tile // CHUNK + 1)
        lax.fori_loop(ready, needed, wait, 0)
        return needed

    return start, wait, wait_until


def local_kernel(
    src_h, dst_h, ids_h, coef_h, feat_h, adj_h,
    acc_ref, held_ref, remote_s,
    feat_ref, adj_ref, src_v, dst_v, ids_s, coef_ref, local_s, entry_v, entry_s, sems, adj_sems,
):
    copies = [
        pltpu.make_async_copy(a, b, sems.at[i])
        for i, (a, b) in enumerate(
            [
                (src_h, src_v), (dst_h, dst_v), (ids_h, ids_s), (coef_h, coef_ref),
                (feat_h, feat_ref), (entry_v, entry_s),
            ]
        )
    ]
    for copy in copies[:-1]:
        copy.start()
    n_tiles = src_v.shape[1]
    n_chunks = n_tiles // CHUNK
    fetch, wait, wait_until = chunked_fetch(adj_h, adj_ref, adj_sems)
    for i in range(EARLY):
        fetch(i, 0)
    group = lax.axis_index("grp")
    group_len = feat_ref.shape[1] // 128
    n_dst = ids_s.shape[0]
    n_grp = lax.axis_size("grp")
    shift = group_len.bit_length() - 1
    copies[0].wait()
    copies[1].wait()
    row = src_v[...]
    src = jnp.broadcast_to(row, (n_grp, n_tiles))
    mine = (src >> shift) == lax.broadcasted_iota(jnp.int32, (n_grp, n_tiles), 0)
    least = four_least(jnp.where(mine, src, BIG))
    rank = jnp.zeros((n_grp, n_tiles), jnp.int32)
    for low in least[: NEED - 1]:
        rank += jnp.where(mine & (src > low), 1, 0)
    slot = (row >> shift) * NEED + jnp.sum(rank, axis=0, keepdims=True)
    head = lax.broadcasted_iota(jnp.int32, (1, n_tiles), 1) + dst_v[...] * 256
    entry_v[...] = head + jnp.where(
        (row >> shift) == group, (row & (group_len - 1)) * 8192 + LOCAL, slot * 8192
    )
    copies[-1].start()
    for i in range(EARLY, n_chunks):
        fetch(i, 0)
    copies[-1].wait()

    def sort_out(t, n_local):
        entry = entry_s[0, t]
        local_s[n_local] = entry
        remote_s[t - n_local] = entry
        return n_local + (entry >> LOCAL_BIT)

    n_local = lax.fori_loop(0, n_tiles, sort_out, 0, unroll=16)
    n_remote = n_tiles - n_local
    for i in range(PAD):
        local_s[n_local + i] = n_dst * 256 + n_tiles - 1
        remote_s[n_remote + i] = n_dst * 256 + n_tiles - 1
    remote_s[remote_s.shape[0] - 1] = n_remote
    copies[2].wait()
    copies[3].wait()
    copies[4].wait()
    for d in range(n_dst):
        place = pl.multiple_of((ids_s[d] - group * group_len) * 128, 128)
        own = feat_ref[:, pl.ds(place, 128)].astype(jnp.float32)
        acc_ref[d] = coef_ref[d : d + 1, :] * own
    acc_ref[n_dst] = jnp.zeros((8, 128), jnp.float32)
    def load_x(place):
        return feat_ref[:, pl.ds(pl.multiple_of(place * 128, 128), 128)].astype(jnp.float32)

    ready = tile_passes(
        local_s, 0, (n_local + BATCH - 1) // BATCH, load_x, lambda _, tile: adj_ref[tile],
        acc_ref, wait_until, 0,
    )
    lax.fori_loop(ready, n_chunks, wait, 0)

    def hold(i, carry):
        held_ref[i] = adj_ref[remote_s[i] & 255]
        return carry

    lax.fori_loop(0, HELD, hold, 0, unroll=8)


def gather_kernel(req_ref, feat_h, out_ref, feat_ref, place_v, place_s, sems):
    fetch = pltpu.make_async_copy(feat_h, feat_ref, sems.at[0])
    fetch.start()
    group = lax.axis_index("grp")
    group_len = feat_ref.shape[1] // 128
    shift = group_len.bit_length() - 1
    n_grp, n_tiles = req_ref.shape
    req = req_ref[...]
    least = four_least(jnp.where((req >> shift) == group, req & (group_len - 1), BIG))
    lane = lax.broadcasted_iota(jnp.int32, (n_grp, 128), 1)
    table = jnp.zeros((n_grp, 128), jnp.int32)
    for r, low in enumerate(least):
        table = jnp.where(lane == r, jnp.minimum(low, group_len - 1), table)
    place_v[...] = table
    copy = pltpu.make_async_copy(place_v, place_s, sems.at[1])
    copy.start()
    copy.wait()
    fetch.wait()
    for k in range(n_grp):
        for r in range(NEED):
            place = pl.multiple_of(place_s[k, r] * 128, 128)
            out_ref[k, r] = feat_ref[:, pl.ds(place, 128)]


def remote_kernel(
    remote_s, recv_ref, acc_in_ref, held_ref, adj_h, out_ref, adj_ref, acc_ref, sems
):
    n_remote = remote_s[remote_s.shape[0] - 1]

    def fetch(i, sem):
        pltpu.make_async_copy(adj_h.at[remote_s[i] & 255], adj_ref.at[i - HELD], sem).start()

    def arrive(first, count, sem):
        tiles = pl.ds(first - HELD, count)
        pltpu.make_async_copy(adj_h.at[pl.ds(0, count)], adj_ref.at[tiles], sem).wait()

    def fetch_pass(step, carry):
        def some(i, c):
            for q in range(FETCH):
                fetch(step * BATCH + i * FETCH + q, sems.at[step])
            return c

        return lax.fori_loop(0, BATCH // FETCH, some, carry)

    n_passes = (n_remote + BATCH - 1) // BATCH
    lax.fori_loop(HELD // BATCH, n_passes, fetch_pass, 0)
    acc_ref[...] = acc_in_ref[...]

    def load_x(slot):
        return recv_ref[slot].astype(jnp.float32)

    def late_pass(step, carry):
        arrive(pl.multiple_of(step * BATCH, BATCH), BATCH, sems.at[step])
        tile_pass(
            remote_s, step * BATCH, BATCH, load_x, lambda index, _: adj_ref[index - HELD], acc_ref
        )
        return carry

    tile_pass(remote_s, 0, HELD, load_x, lambda index, _: held_ref[index], acc_ref)
    lax.fori_loop(HELD // BATCH, n_passes, late_pass, 0)
    out_ref[...] = acc_ref[: out_ref.shape[0]].astype(out_ref.dtype)


def per_device(features, adj_tiles, tile_dst, tile_src, dst_ids, self_coef, weight, out_bias):
    n_feat = features.shape[0]
    n_tiles = tile_src.shape[0]
    n_dst = dst_ids.shape[0]
    n_grp = lax.axis_size("grp")
    n_slots = n_grp * NEED
    params = pltpu.CompilerParams(vmem_limit_bytes=16 << 20)
    requests = lax.all_to_all(
        jnp.broadcast_to(tile_src, (n_grp, n_tiles)), "grp", 0, 0, tiled=True
    )
    acc, adj_held, remote = pl.pallas_call(
        local_kernel,
        name="local",
        out_shape=(
            pltpu.VMEM((n_dst + 1, n_feat, 128), jnp.float32),
            pltpu.VMEM((HELD,) + adj_tiles.shape[1:], adj_tiles.dtype),
            pltpu.SMEM((n_tiles + PAD + 1,), jnp.int32),
        ),
        in_specs=[HBM] * 6,
        out_specs=(VMEM, VMEM, SMEM),
        scratch_shapes=[
            pltpu.VMEM(features.shape, features.dtype),
            pltpu.VMEM(adj_tiles.shape, adj_tiles.dtype),
            pltpu.VMEM((1, n_tiles), jnp.int32),
            pltpu.VMEM((1, n_tiles), jnp.int32),
            pltpu.SMEM((n_dst,), jnp.int32),
            pltpu.VMEM((n_dst, 128), jnp.float32),
            pltpu.SMEM((n_tiles + PAD,), jnp.int32),
            pltpu.VMEM((1, n_tiles), jnp.int32),
            pltpu.SMEM((1, n_tiles), jnp.int32),
            pltpu.SemaphoreType.DMA((6,)),
            pltpu.SemaphoreType.DMA((n_tiles // CHUNK,)),
        ],
        compiler_params=params,
        cost_estimate=pl.CostEstimate(
            flops=2 * n_tiles * 128 * 128 * 32, bytes_accessed=18 << 20, transcendentals=0
        ),
    )(
        *[
            pltpu.with_memory_space_constraint(a, pltpu.HBM)
            for a in (
                tile_src.reshape(1, n_tiles), tile_dst.reshape(1, n_tiles), dst_ids,
                self_coef.reshape(n_dst, 128), features, adj_tiles,
            )
        ]
    )
    blocks = pl.pallas_call(
        gather_kernel,
        name="gather",
        out_shape=jax.ShapeDtypeStruct((n_grp, NEED, n_feat, 128), features.dtype),
        in_specs=[VMEM, HBM],
        out_specs=VMEM,
        scratch_shapes=[
            pltpu.VMEM(features.shape, features.dtype),
            pltpu.VMEM((n_grp, 128), jnp.int32),
            pltpu.SMEM((n_grp, 128), jnp.int32),
            pltpu.SemaphoreType.DMA((2,)),
        ],
        compiler_params=params,
    )(requests, pltpu.with_memory_space_constraint(features, pltpu.HBM))
    arrived = lax.all_to_all(blocks, "grp", 0, 0, tiled=True).reshape(n_slots, n_feat, 128)
    aggregated = pl.pallas_call(
        remote_kernel,
        name="remote",
        out_shape=jax.ShapeDtypeStruct((n_dst, n_feat, 128), jnp.bfloat16),
        in_specs=[SMEM, VMEM, VMEM, VMEM, HBM],
        out_specs=VMEM,
        scratch_shapes=[
            pltpu.VMEM((n_tiles - HELD,) + adj_tiles.shape[1:], adj_tiles.dtype),
            pltpu.VMEM((n_dst + 1, n_feat, 128), jnp.float32),
            pltpu.SemaphoreType.DMA((n_tiles // BATCH,)),
        ],
        compiler_params=params,
    )(
        remote, arrived, pltpu.with_memory_space_constraint(acc, pltpu.VMEM),
        pltpu.with_memory_space_constraint(adj_held, pltpu.VMEM),
        pltpu.with_memory_space_constraint(adj_tiles, pltpu.HBM),
    )
    rows = lax.all_to_all(aggregated, "col", 0, 0, tiled=True).reshape(-1, 128)
    mixed = (
        lax.dot_general(
            rows, weight, (((0,), (0,)), ((), ())), preferred_element_type=jnp.float32
        )
        + out_bias
    )
    return jax.nn.relu(mixed).astype(jnp.bfloat16)


def solution(mesh):
    in_specs = (
        P("col", "grp"),
        P("grp", None, None),
        P("grp"),
        P("grp"),
        P("grp"),
        P("grp"),
        P(),
        P(),
    )
    out_specs = P(("grp", "col"), None)
    return jax.shard_map(
        per_device, mesh=mesh, in_specs=in_specs, out_specs=out_specs, check_vma=False
    )
```

```python
import jax
import jax.numpy as jnp
from jax import lax
from jax.experimental import pallas as pl
from jax.experimental.pallas import tpu as pltpu
from jax.sharding import PartitionSpec as P

NEED = 4
BATCH = 32
HELD = 96
LATE = 40
FETCH = 8
PAD = 40
CHUNK = 16
EARLY = 2
BIG = 1 << 30
LOCAL_BIT = 24
LOCAL = 1 << LOCAL_BIT

VMEM = pl.BlockSpec(memory_space=pltpu.VMEM)
SMEM = pl.BlockSpec(memory_space=pltpu.SMEM)
HBM = pl.BlockSpec(memory_space=pltpu.HBM)


def four_least(values):
    values = values.astype(jnp.float32)
    least = []
    for _ in range(NEED):
        low = jnp.min(values, axis=1, keepdims=True)
        least.append(low.astype(jnp.int32))
        values = jnp.where(values > low, values, float(BIG))
    return least


def tile_pass(entries, first, count, load_x, load_tile, acc_ref):
    zero = jnp.zeros((8, 128), jnp.float32)
    results = []
    for pair in range(count // 2):
        tiles, xs, dsts = [], [], []
        for q in range(2):
            index = first + pair * 2 + q
            entry = entries[index]
            tiles.append(load_tile(index, entry & 255))
            xs.append(load_x((entry >> 13) & 2047))
            dsts.append((entry >> 8) & 31)
        left = jnp.concatenate([xs[0], zero], axis=0)
        right = jnp.concatenate([zero, xs[1]], axis=0)
        lhs = jnp.concatenate([left, right], axis=1).astype(jnp.bfloat16)
        rhs = jnp.concatenate(tiles, axis=1)
        out = lax.dot_general(
            lhs, rhs, (((1,), (1,)), ((), ())), preferred_element_type=jnp.float32
        )
        results += [(dsts[0], out[0:8]), (dsts[1], out[8:16])]
    for dst, value in results:
        acc_ref[dst] += value


def tile_passes(entries, first, last, load_x, load_tile, acc_ref, wait_until, ready):
    def one_pass(step, ready):
        ready = wait_until(entries[step * BATCH + BATCH - 1] & 255, ready)
        tile_pass(entries, step * BATCH, BATCH, load_x, load_tile, acc_ref)
        return ready

    return lax.fori_loop(first, last, one_pass, ready)


def chunked_fetch(adj_h, adj_ref, sems):
    def chunk(i):
        tiles = pl.ds(pl.multiple_of(i * CHUNK, CHUNK), CHUNK)
        return pltpu.make_async_copy(adj_h.at[tiles], adj_ref.at[tiles], sems.at[i])

    def start(i, carry):
        chunk(i).start()
        return carry

    def wait(i, carry):
        chunk(i).wait()
        return carry

    def wait_until(tile, ready):
        needed = jnp.maximum(ready, tile // CHUNK + 1)
        lax.fori_loop(ready, needed, wait, 0)
        return needed

    return start, wait, wait_until


def local_kernel(
    src_h, dst_h, ids_h, coef_h, feat_h, adj_h,
    acc_ref, held_ref, remote_s,
    feat_ref, adj_ref, src_v, dst_v, ids_s, coef_ref, local_s, entry_v, entry_s, sems, adj_sems,
):
    copies = [
        pltpu.make_async_copy(a, b, sems.at[i])
        for i, (a, b) in enumerate(
            [
                (src_h, src_v), (dst_h, dst_v), (ids_h, ids_s), (coef_h, coef_ref),
                (feat_h, feat_ref), (entry_v, entry_s),
            ]
        )
    ]
    for copy in copies[:-1]:
        copy.start()
    n_tiles = src_v.shape[1]
    n_chunks = n_tiles // CHUNK
    fetch, wait, wait_until = chunked_fetch(adj_h, adj_ref, adj_sems)
    for i in range(EARLY):
        fetch(i, 0)
    group = lax.axis_index("grp")
    group_len = feat_ref.shape[1] // 128
    n_dst = ids_s.shape[0]
    n_grp = lax.axis_size("grp")
    shift = group_len.bit_length() - 1
    copies[0].wait()
    copies[1].wait()
    row = src_v[...]
    src = jnp.broadcast_to(row, (n_grp, n_tiles))
    mine = (src >> shift) == lax.broadcasted_iota(jnp.int32, (n_grp, n_tiles), 0)
    least = four_least(jnp.where(mine, src, BIG))
    rank = jnp.zeros((n_grp, n_tiles), jnp.int32)
    for low in least[: NEED - 1]:
        rank += jnp.where(mine & (src > low), 1, 0)
    slot = (row >> shift) * NEED + jnp.sum(rank, axis=0, keepdims=True)
    head = lax.broadcasted_iota(jnp.int32, (1, n_tiles), 1) + dst_v[...] * 256
    entry_v[...] = head + jnp.where(
        (row >> shift) == group, (row & (group_len - 1)) * 8192 + LOCAL, slot * 8192
    )
    copies[-1].start()
    for i in range(EARLY, n_chunks):
        fetch(i, 0)
    copies[-1].wait()

    def sort_out(t, n_local):
        entry = entry_s[0, t]
        local_s[n_local] = entry
        remote_s[t - n_local] = entry
        return n_local + (entry >> LOCAL_BIT)

    n_local = lax.fori_loop(0, n_tiles, sort_out, 0, unroll=16)
    n_remote = n_tiles - n_local
    for i in range(PAD):
        local_s[n_local + i] = n_dst * 256 + n_tiles - 1
        remote_s[n_remote + i] = n_dst * 256 + n_tiles - PAD + i
    remote_s[remote_s.shape[0] - 1] = n_remote
    copies[2].wait()
    copies[3].wait()
    copies[4].wait()
    for d in range(n_dst):
        place = pl.multiple_of((ids_s[d] - group * group_len) * 128, 128)
        own = feat_ref[:, pl.ds(place, 128)].astype(jnp.float32)
        acc_ref[d] = coef_ref[d : d + 1, :] * own
    acc_ref[n_dst] = jnp.zeros((8, 128), jnp.float32)
    def load_x(place):
        return feat_ref[:, pl.ds(pl.multiple_of(place * 128, 128), 128)].astype(jnp.float32)

    ready = tile_passes(
        local_s, 0, (n_local + BATCH - 1) // BATCH, load_x, lambda _, tile: adj_ref[tile],
        acc_ref, wait_until, 0,
    )
    lax.fori_loop(ready, n_chunks, wait, 0)

    def hold(i, carry):
        held_ref[i] = adj_ref[remote_s[i] & 255]
        return carry

    lax.fori_loop(0, HELD, hold, 0, unroll=8)


def spread_kernel(src_h, feat_h, out_ref, feat_ref, src_v, sems):
    copy = pltpu.make_async_copy(src_h, src_v, sems.at[0])
    copy.start()
    fetch = pltpu.make_async_copy(feat_h, feat_ref, sems.at[1])
    fetch.start()
    copy.wait()
    out_ref[...] = jnp.broadcast_to(src_v[...][None], out_ref.shape)
    fetch.wait()


def gather_kernel(req_ref, feat_ref, out_ref):
    group = lax.axis_index("grp")
    group_len = feat_ref.shape[1] // 128
    shift = group_len.bit_length() - 1
    req = req_ref[...]
    least = four_least(jnp.where((req >> shift) == group, req & (group_len - 1), BIG))
    lane = lax.broadcasted_iota(jnp.int32, (req.shape[0], 128), 1)
    table = jnp.zeros((req.shape[0], 128), jnp.int32)
    for r, low in enumerate(least):
        table = jnp.where(lane == r, jnp.minimum(low, group_len - 1), table)
    for k in range(req.shape[0]):
        for r in range(NEED):
            place = pl.multiple_of(table[k, r] * 128, 128)
            out_ref[k, r] = feat_ref[:, pl.ds(place, 128)]


def remote_kernel(
    remote_s, recv_ref, acc_in_ref, held_ref, adj_h, out_ref, adj_ref, acc_ref, sems
):
    n_remote = remote_s[remote_s.shape[0] - 1]

    n_passes = (jnp.maximum(n_remote - HELD, 0) + LATE - 1) // LATE

    def fetch_some(i, step):
        for q in range(FETCH):
            place = step * LATE + i * FETCH + q
            pltpu.make_async_copy(
                adj_h.at[remote_s[HELD + place] & 255], adj_ref.at[place], sems.at[step]
            ).start()
        return step

    def fetch_pass(step, carry):
        lax.fori_loop(0, LATE // FETCH, fetch_some, step)
        return carry

    lax.fori_loop(0, n_passes, fetch_pass, 0)
    acc_ref[...] = acc_in_ref[...]

    def load_x(slot):
        return recv_ref[slot].astype(jnp.float32)

    def late_pass(step, carry):
        first = pl.multiple_of(step * LATE, LATE)
        pltpu.make_async_copy(
            adj_h.at[pl.ds(0, LATE)], adj_ref.at[pl.ds(first, LATE)], sems.at[step]
        ).wait()
        tile_pass(
            remote_s, HELD + first, LATE, load_x, lambda index, _: adj_ref[index - HELD], acc_ref
        )
        return carry

    tile_pass(remote_s, 0, HELD, load_x, lambda index, _: held_ref[index], acc_ref)
    lax.fori_loop(0, n_passes, late_pass, 0)
    out_ref[...] = acc_ref[: out_ref.shape[0]].astype(out_ref.dtype)


def per_device(features, adj_tiles, tile_dst, tile_src, dst_ids, self_coef, weight, out_bias):
    n_feat = features.shape[0]
    n_tiles = tile_src.shape[0]
    n_dst = dst_ids.shape[0]
    n_grp = lax.axis_size("grp")
    n_slots = n_grp * NEED
    params = pltpu.CompilerParams(vmem_limit_bytes=16 << 20)
    spread, feat_held = pl.pallas_call(
        spread_kernel,
        name="spread",
        out_shape=(
            pltpu.VMEM((n_grp, 1, n_tiles), jnp.int32),
            pltpu.VMEM(features.shape, features.dtype),
        ),
        in_specs=[HBM, HBM],
        out_specs=(VMEM, VMEM),
        scratch_shapes=[pltpu.VMEM((1, n_tiles), jnp.int32), pltpu.SemaphoreType.DMA((2,))],
        compiler_params=pltpu.CompilerParams(vmem_limit_bytes=4 << 20),
    )(
        pltpu.with_memory_space_constraint(tile_src.reshape(1, n_tiles), pltpu.HBM),
        pltpu.with_memory_space_constraint(features, pltpu.HBM),
    )
    requests = lax.all_to_all(spread, "grp", 0, 0, tiled=True).reshape(n_grp, n_tiles)
    acc, adj_held, remote = pl.pallas_call(
        local_kernel,
        name="local",
        out_shape=(
            pltpu.VMEM((n_dst + 1, n_feat, 128), jnp.float32),
            pltpu.VMEM((HELD,) + adj_tiles.shape[1:], adj_tiles.dtype),
            pltpu.SMEM((n_tiles + PAD + 1,), jnp.int32),
        ),
        in_specs=[HBM] * 6,
        out_specs=(VMEM, VMEM, SMEM),
        scratch_shapes=[
            pltpu.VMEM(features.shape, features.dtype),
            pltpu.VMEM(adj_tiles.shape, adj_tiles.dtype),
            pltpu.VMEM((1, n_tiles), jnp.int32),
            pltpu.VMEM((1, n_tiles), jnp.int32),
            pltpu.SMEM((n_dst,), jnp.int32),
            pltpu.VMEM((n_dst, 128), jnp.float32),
            pltpu.SMEM((n_tiles + PAD,), jnp.int32),
            pltpu.VMEM((1, n_tiles), jnp.int32),
            pltpu.SMEM((1, n_tiles), jnp.int32),
            pltpu.SemaphoreType.DMA((6,)),
            pltpu.SemaphoreType.DMA((n_tiles // CHUNK,)),
        ],
        compiler_params=params,
        cost_estimate=pl.CostEstimate(
            flops=2 * n_tiles * 128 * 128 * 32, bytes_accessed=18 << 20, transcendentals=0
        ),
    )(
        *[
            pltpu.with_memory_space_constraint(a, pltpu.HBM)
            for a in (
                tile_src.reshape(1, n_tiles), tile_dst.reshape(1, n_tiles), dst_ids,
                self_coef.reshape(n_dst, 128), features, adj_tiles,
            )
        ]
    )
    blocks = pl.pallas_call(
        gather_kernel,
        name="gather",
        out_shape=jax.ShapeDtypeStruct((n_grp, NEED, n_feat, 128), features.dtype),
        in_specs=[VMEM, VMEM],
        out_specs=VMEM,
        compiler_params=pltpu.CompilerParams(vmem_limit_bytes=4 << 20),
    )(requests, pltpu.with_memory_space_constraint(feat_held, pltpu.VMEM))
    arrived = lax.all_to_all(blocks, "grp", 0, 0, tiled=True).reshape(n_slots, n_feat, 128)
    aggregated = pl.pallas_call(
        remote_kernel,
        name="remote",
        out_shape=jax.ShapeDtypeStruct((n_dst, n_feat, 128), jnp.bfloat16),
        in_specs=[SMEM, VMEM, VMEM, VMEM, HBM],
        out_specs=VMEM,
        scratch_shapes=[
            pltpu.VMEM((n_tiles - HELD,) + adj_tiles.shape[1:], adj_tiles.dtype),
            pltpu.VMEM((n_dst + 1, n_feat, 128), jnp.float32),
            pltpu.SemaphoreType.DMA(((n_tiles - HELD) // LATE,)),
        ],
        compiler_params=params,
    )(
        remote, arrived, pltpu.with_memory_space_constraint(acc, pltpu.VMEM),
        pltpu.with_memory_space_constraint(adj_held, pltpu.VMEM),
        pltpu.with_memory_space_constraint(adj_tiles, pltpu.HBM),
    )
    rows = lax.all_to_all(aggregated, "col", 0, 0, tiled=True).reshape(-1, 128)
    mixed = (
        lax.dot_general(
            rows, weight, (((0,), (0,)), ((), ())), preferred_element_type=jnp.float32
        )
        + out_bias
    )
    return jax.nn.relu(mixed).astype(jnp.bfloat16)


def solution(mesh):
    in_specs = (
        P("col", "grp"),
        P("grp", None, None),
        P("grp"),
        P("grp"),
        P("grp"),
        P("grp"),
        P(),
        P(),
    )
    out_specs = P(("grp", "col"), None)
    return jax.shard_map(
        per_device, mesh=mesh, in_specs=in_specs, out_specs=out_specs, check_vma=False
    )
```

```python
import jax
import jax.numpy as jnp
from jax import lax
from jax.experimental import pallas as pl
from jax.experimental.pallas import tpu as pltpu
from jax.sharding import PartitionSpec as P

NEED = 4
BATCH = 32
HELD = 100
LATE = 36
FETCH = 12
PAD = 40
CHUNK = 16
EARLY = 2
BIG = 1 << 30
LOCAL_BIT = 24
LOCAL = 1 << LOCAL_BIT

VMEM = pl.BlockSpec(memory_space=pltpu.VMEM)
SMEM = pl.BlockSpec(memory_space=pltpu.SMEM)
HBM = pl.BlockSpec(memory_space=pltpu.HBM)


def four_least(values):
    values = values.astype(jnp.float32)
    least = []
    for _ in range(NEED):
        low = jnp.min(values, axis=1, keepdims=True)
        least.append(low.astype(jnp.int32))
        values = jnp.where(values > low, values, float(BIG))
    return least


def tile_pass(entries, first, count, load_x, load_tile, acc_ref):
    zero = jnp.zeros((8, 128), jnp.float32)
    results = []
    for pair in range(count // 2):
        tiles, xs, dsts = [], [], []
        for q in range(2):
            index = first + pair * 2 + q
            entry = entries[index]
            tiles.append(load_tile(index, entry & 255))
            xs.append(load_x((entry >> 13) & 2047))
            dsts.append((entry >> 8) & 31)
        left = jnp.concatenate([xs[0], zero], axis=0)
        right = jnp.concatenate([zero, xs[1]], axis=0)
        lhs = jnp.concatenate([left, right], axis=1).astype(jnp.bfloat16)
        rhs = jnp.concatenate(tiles, axis=1)
        out = lax.dot_general(
            lhs, rhs, (((1,), (1,)), ((), ())), preferred_element_type=jnp.float32
        )
        results += [(dsts[0], out[0:8]), (dsts[1], out[8:16])]
    for dst, value in results:
        acc_ref[dst] += value


def tile_passes(entries, first, last, load_x, load_tile, acc_ref, wait_until, ready):
    def one_pass(step, ready):
        ready = wait_until(entries[step * BATCH + BATCH - 1] & 255, ready)
        tile_pass(entries, step * BATCH, BATCH, load_x, load_tile, acc_ref)
        return ready

    return lax.fori_loop(first, last, one_pass, ready)


def chunked_fetch(adj_h, adj_ref, sems):
    def chunk(i):
        tiles = pl.ds(pl.multiple_of(i * CHUNK, CHUNK), CHUNK)
        return pltpu.make_async_copy(adj_h.at[tiles], adj_ref.at[tiles], sems.at[i])

    def start(i, carry):
        chunk(i).start()
        return carry

    def wait(i, carry):
        chunk(i).wait()
        return carry

    def wait_until(tile, ready):
        needed = jnp.maximum(ready, tile // CHUNK + 1)
        lax.fori_loop(ready, needed, wait, 0)
        return needed

    return start, wait, wait_until


def local_kernel(
    src_h, dst_h, ids_h, coef_h, feat_h, adj_h,
    acc_ref, held_ref, remote_s,
    feat_ref, adj_ref, src_v, dst_v, ids_s, coef_ref, local_s, entry_v, entry_s, sems, adj_sems,
):
    copies = [
        pltpu.make_async_copy(a, b, sems.at[i])
        for i, (a, b) in enumerate(
            [
                (src_h, src_v), (dst_h, dst_v), (ids_h, ids_s), (coef_h, coef_ref),
                (feat_h, feat_ref), (entry_v, entry_s),
            ]
        )
    ]
    for copy in copies[:-1]:
        copy.start()
    n_tiles = src_v.shape[1]
    n_chunks = n_tiles // CHUNK
    fetch, wait, wait_until = chunked_fetch(adj_h, adj_ref, adj_sems)
    for i in range(EARLY):
        fetch(i, 0)
    group = lax.axis_index("grp")
    group_len = feat_ref.shape[1] // 128
    n_dst = ids_s.shape[0]
    n_grp = lax.axis_size("grp")
    shift = group_len.bit_length() - 1
    copies[0].wait()
    copies[1].wait()
    row = src_v[...]
    src = jnp.broadcast_to(row, (n_grp, n_tiles))
    mine = (src >> shift) == lax.broadcasted_iota(jnp.int32, (n_grp, n_tiles), 0)
    least = four_least(jnp.where(mine, src, BIG))
    rank = jnp.zeros((n_grp, n_tiles), jnp.int32)
    for low in least[: NEED - 1]:
        rank += jnp.where(mine & (src > low), 1, 0)
    slot = (row >> shift) * NEED + jnp.sum(rank, axis=0, keepdims=True)
    head = lax.broadcasted_iota(jnp.int32, (1, n_tiles), 1) + dst_v[...] * 256
    entry_v[...] = head + jnp.where(
        (row >> shift) == group, (row & (group_len - 1)) * 8192 + LOCAL, slot * 8192
    )
    copies[-1].start()
    for i in range(EARLY, n_chunks):
        fetch(i, 0)
    copies[-1].wait()

    def sort_out(t, n_local):
        entry = entry_s[0, t]
        local_s[n_local] = entry
        remote_s[t - n_local] = entry
        return n_local + (entry >> LOCAL_BIT)

    n_local = lax.fori_loop(0, n_tiles, sort_out, 0, unroll=16)
    n_remote = n_tiles - n_local
    for i in range(PAD):
        local_s[n_local + i] = n_dst * 256 + n_tiles - 1
        remote_s[n_remote + i] = n_dst * 256 + n_tiles - PAD + i
    remote_s[remote_s.shape[0] - 1] = n_remote
    copies[2].wait()
    copies[3].wait()
    copies[4].wait()
    for d in range(n_dst):
        place = pl.multiple_of((ids_s[d] - group * group_len) * 128, 128)
        own = feat_ref[:, pl.ds(place, 128)].astype(jnp.float32)
        acc_ref[d] = coef_ref[d : d + 1, :] * own
    acc_ref[n_dst] = jnp.zeros((8, 128), jnp.float32)
    def load_x(place):
        return feat_ref[:, pl.ds(pl.multiple_of(place * 128, 128), 128)].astype(jnp.float32)

    ready = tile_passes(
        local_s, 0, (n_local + BATCH - 1) // BATCH, load_x, lambda _, tile: adj_ref[tile],
        acc_ref, wait_until, 0,
    )
    lax.fori_loop(ready, n_chunks, wait, 0)

    def hold(i, carry):
        held_ref[i] = adj_ref[remote_s[i] & 255]
        return carry

    lax.fori_loop(0, HELD, hold, 0, unroll=8)


def spread_kernel(src_h, feat_h, out_ref, feat_ref, src_v, sems):
    copy = pltpu.make_async_copy(src_h, src_v, sems.at[0])
    copy.start()
    fetch = pltpu.make_async_copy(feat_h, feat_ref, sems.at[1])
    fetch.start()
    copy.wait()
    out_ref[...] = jnp.broadcast_to(src_v[...][None], out_ref.shape)
    fetch.wait()


def gather_kernel(req_ref, feat_ref, out_ref):
    group = lax.axis_index("grp")
    group_len = feat_ref.shape[1] // 128
    shift = group_len.bit_length() - 1
    req = req_ref[...]
    least = four_least(jnp.where((req >> shift) == group, req & (group_len - 1), BIG))
    lane = lax.broadcasted_iota(jnp.int32, (req.shape[0], 128), 1)
    table = jnp.zeros((req.shape[0], 128), jnp.int32)
    for r, low in enumerate(least):
        table = jnp.where(lane == r, jnp.minimum(low, group_len - 1), table)
    for k in range(req.shape[0]):
        for r in range(NEED):
            place = pl.multiple_of(table[k, r] * 128, 128)
            out_ref[k, r] = feat_ref[:, pl.ds(place, 128)]


def remote_kernel(
    remote_s, recv_ref, acc_in_ref, held_ref, adj_h, out_ref, adj_ref, acc_ref, sems
):
    n_remote = remote_s[remote_s.shape[0] - 1]

    n_passes = (jnp.maximum(n_remote - HELD, 0) + LATE - 1) // LATE

    def fetch_some(i, step):
        for q in range(FETCH):
            place = step * LATE + i * FETCH + q
            pltpu.make_async_copy(
                adj_h.at[remote_s[HELD + place] & 255], adj_ref.at[place], sems.at[step]
            ).start()
        return step

    def fetch_pass(step, carry):
        lax.fori_loop(0, LATE // FETCH, fetch_some, step)
        return carry

    lax.fori_loop(0, n_passes, fetch_pass, 0)
    acc_ref[...] = acc_in_ref[...]

    def load_x(slot):
        return recv_ref[slot].astype(jnp.float32)

    def late_pass(step, carry):
        first = pl.multiple_of(step * LATE, LATE)
        pltpu.make_async_copy(
            adj_h.at[pl.ds(0, LATE)], adj_ref.at[pl.ds(first, LATE)], sems.at[step]
        ).wait()
        tile_pass(
            remote_s, HELD + first, LATE, load_x, lambda index, _: adj_ref[index - HELD], acc_ref
        )
        return carry

    tile_pass(remote_s, 0, HELD, load_x, lambda index, _: held_ref[index], acc_ref)
    lax.fori_loop(0, n_passes, late_pass, 0)
    out_ref[...] = acc_ref[: out_ref.shape[0]].astype(out_ref.dtype)


def per_device(features, adj_tiles, tile_dst, tile_src, dst_ids, self_coef, weight, out_bias):
    n_feat = features.shape[0]
    n_tiles = tile_src.shape[0]
    n_dst = dst_ids.shape[0]
    n_grp = lax.axis_size("grp")
    n_slots = n_grp * NEED
    params = pltpu.CompilerParams(vmem_limit_bytes=16 << 20)
    spread, feat_held = pl.pallas_call(
        spread_kernel,
        name="spread",
        out_shape=(
            pltpu.VMEM((n_grp, 1, n_tiles), jnp.int32),
            pltpu.VMEM(features.shape, features.dtype),
        ),
        in_specs=[HBM, HBM],
        out_specs=(VMEM, VMEM),
        scratch_shapes=[pltpu.VMEM((1, n_tiles), jnp.int32), pltpu.SemaphoreType.DMA((2,))],
        compiler_params=pltpu.CompilerParams(vmem_limit_bytes=4 << 20),
    )(
        pltpu.with_memory_space_constraint(tile_src.reshape(1, n_tiles), pltpu.HBM),
        pltpu.with_memory_space_constraint(features, pltpu.HBM),
    )
    requests = lax.all_to_all(spread, "grp", 0, 0, tiled=True).reshape(n_grp, n_tiles)
    acc, adj_held, remote = pl.pallas_call(
        local_kernel,
        name="local",
        out_shape=(
            pltpu.VMEM((n_dst + 1, n_feat, 128), jnp.float32),
            pltpu.VMEM((HELD,) + adj_tiles.shape[1:], adj_tiles.dtype),
            pltpu.SMEM((n_tiles + PAD + 1,), jnp.int32),
        ),
        in_specs=[HBM] * 6,
        out_specs=(VMEM, VMEM, SMEM),
        scratch_shapes=[
            pltpu.VMEM(features.shape, features.dtype),
            pltpu.VMEM(adj_tiles.shape, adj_tiles.dtype),
            pltpu.VMEM((1, n_tiles), jnp.int32),
            pltpu.VMEM((1, n_tiles), jnp.int32),
            pltpu.SMEM((n_dst,), jnp.int32),
            pltpu.VMEM((n_dst, 128), jnp.float32),
            pltpu.SMEM((n_tiles + PAD,), jnp.int32),
            pltpu.VMEM((1, n_tiles), jnp.int32),
            pltpu.SMEM((1, n_tiles), jnp.int32),
            pltpu.SemaphoreType.DMA((6,)),
            pltpu.SemaphoreType.DMA((n_tiles // CHUNK,)),
        ],
        compiler_params=params,
        cost_estimate=pl.CostEstimate(
            flops=2 * n_tiles * 128 * 128 * 32, bytes_accessed=18 << 20, transcendentals=0
        ),
    )(
        *[
            pltpu.with_memory_space_constraint(a, pltpu.HBM)
            for a in (
                tile_src.reshape(1, n_tiles), tile_dst.reshape(1, n_tiles), dst_ids,
                self_coef.reshape(n_dst, 128), features, adj_tiles,
            )
        ]
    )
    blocks = pl.pallas_call(
        gather_kernel,
        name="gather",
        out_shape=jax.ShapeDtypeStruct((n_grp, NEED, n_feat, 128), features.dtype),
        in_specs=[VMEM, VMEM],
        out_specs=VMEM,
        compiler_params=pltpu.CompilerParams(vmem_limit_bytes=4 << 20),
    )(requests, pltpu.with_memory_space_constraint(feat_held, pltpu.VMEM))
    arrived = lax.all_to_all(blocks, "grp", 0, 0, tiled=True).reshape(n_slots, n_feat, 128)
    aggregated = pl.pallas_call(
        remote_kernel,
        name="remote",
        out_shape=jax.ShapeDtypeStruct((n_dst, n_feat, 128), jnp.bfloat16),
        in_specs=[SMEM, VMEM, VMEM, VMEM, HBM],
        out_specs=VMEM,
        scratch_shapes=[
            pltpu.VMEM((-(-(n_tiles - HELD) // LATE) * LATE,) + adj_tiles.shape[1:], adj_tiles.dtype),
            pltpu.VMEM((n_dst + 1, n_feat, 128), jnp.float32),
            pltpu.SemaphoreType.DMA((-(-(n_tiles - HELD) // LATE),)),
        ],
        compiler_params=params,
    )(
        remote, arrived, pltpu.with_memory_space_constraint(acc, pltpu.VMEM),
        pltpu.with_memory_space_constraint(adj_held, pltpu.VMEM),
        pltpu.with_memory_space_constraint(adj_tiles, pltpu.HBM),
    )
    rows = lax.all_to_all(aggregated, "col", 0, 0, tiled=True).reshape(-1, 128)
    mixed = (
        lax.dot_general(
            rows, weight, (((0,), (0,)), ((), ())), preferred_element_type=jnp.float32
        )
        + out_bias
    )
    return jax.nn.relu(mixed).astype(jnp.bfloat16)


def solution(mesh):
    in_specs = (
        P("col", "grp"),
        P("grp", None, None),
        P("grp"),
        P("grp"),
        P("grp"),
        P("grp"),
        P(),
        P(),
    )
    out_specs = P(("grp", "col"), None)
    return jax.shard_map(
        per_device, mesh=mesh, in_specs=in_specs, out_specs=out_specs, check_vma=False
    )
```

```python
import jax
import jax.numpy as jnp
from jax import lax
from jax.experimental import pallas as pl
from jax.experimental.pallas import tpu as pltpu
from jax.sharding import PartitionSpec as P

NEED = 4
BATCH = 32
HELD = 100
LATE = 30
FETCH = 10
PAD = 40
CHUNK = 16
EARLY = 2
BIG = 1 << 30
LOCAL_BIT = 24
LOCAL = 1 << LOCAL_BIT

VMEM = pl.BlockSpec(memory_space=pltpu.VMEM)
SMEM = pl.BlockSpec(memory_space=pltpu.SMEM)
HBM = pl.BlockSpec(memory_space=pltpu.HBM)


def four_least(values):
    values = values.astype(jnp.float32)
    least = []
    for _ in range(NEED):
        low = jnp.min(values, axis=1, keepdims=True)
        least.append(low.astype(jnp.int32))
        values = jnp.where(values > low, values, float(BIG))
    return least


def tile_pass(entries, first, count, load_x, load_tile, acc_ref):
    zero = jnp.zeros((8, 128), jnp.float32)
    results = []
    for pair in range(count // 2):
        tiles, xs, dsts = [], [], []
        for q in range(2):
            index = first + pair * 2 + q
            entry = entries[index]
            tiles.append(load_tile(index, entry & 255))
            xs.append(load_x((entry >> 13) & 2047))
            dsts.append((entry >> 8) & 31)
        left = jnp.concatenate([xs[0], zero], axis=0)
        right = jnp.concatenate([zero, xs[1]], axis=0)
        lhs = jnp.concatenate([left, right], axis=1).astype(jnp.bfloat16)
        rhs = jnp.concatenate(tiles, axis=1)
        out = lax.dot_general(
            lhs, rhs, (((1,), (1,)), ((), ())), preferred_element_type=jnp.float32
        )
        results += [(dsts[0], out[0:8]), (dsts[1], out[8:16])]
    for dst, value in results:
        acc_ref[dst] += value


def tile_passes(entries, first, last, load_x, load_tile, acc_ref, wait_until, ready):
    def one_pass(step, ready):
        ready = wait_until(entries[step * BATCH + BATCH - 1] & 255, ready)
        tile_pass(entries, step * BATCH, BATCH, load_x, load_tile, acc_ref)
        return ready

    return lax.fori_loop(first, last, one_pass, ready)


def chunked_fetch(adj_h, adj_ref, sems):
    def chunk(i):
        tiles = pl.ds(pl.multiple_of(i * CHUNK, CHUNK), CHUNK)
        return pltpu.make_async_copy(adj_h.at[tiles], adj_ref.at[tiles], sems.at[i])

    def start(i, carry):
        chunk(i).start()
        return carry

    def wait(i, carry):
        chunk(i).wait()
        return carry

    def wait_until(tile, ready):
        needed = jnp.maximum(ready, tile // CHUNK + 1)
        lax.fori_loop(ready, needed, wait, 0)
        return needed

    return start, wait, wait_until


def local_kernel(
    src_h, dst_h, ids_h, coef_h, feat_h, adj_h,
    acc_ref, held_ref, remote_s,
    feat_ref, adj_ref, src_v, dst_v, ids_s, coef_ref, local_s, entry_v, entry_s, sems, adj_sems,
):
    copies = [
        pltpu.make_async_copy(a, b, sems.at[i])
        for i, (a, b) in enumerate(
            [
                (src_h, src_v), (dst_h, dst_v), (ids_h, ids_s), (coef_h, coef_ref),
                (feat_h, feat_ref), (entry_v, entry_s),
            ]
        )
    ]
    for copy in copies[:-1]:
        copy.start()
    n_tiles = src_v.shape[1]
    n_chunks = n_tiles // CHUNK
    fetch, wait, wait_until = chunked_fetch(adj_h, adj_ref, adj_sems)
    for i in range(EARLY):
        fetch(i, 0)
    group = lax.axis_index("grp")
    group_len = feat_ref.shape[1] // 128
    n_dst = ids_s.shape[0]
    n_grp = lax.axis_size("grp")
    shift = group_len.bit_length() - 1
    copies[0].wait()
    copies[1].wait()
    row = src_v[...]
    src = jnp.broadcast_to(row, (n_grp, n_tiles))
    mine = (src >> shift) == lax.broadcasted_iota(jnp.int32, (n_grp, n_tiles), 0)
    least = four_least(jnp.where(mine, src, BIG))
    rank = jnp.zeros((n_grp, n_tiles), jnp.int32)
    for low in least[: NEED - 1]:
        rank += jnp.where(mine & (src > low), 1, 0)
    slot = (row >> shift) * NEED + jnp.sum(rank, axis=0, keepdims=True)
    head = lax.broadcasted_iota(jnp.int32, (1, n_tiles), 1) + dst_v[...] * 256
    entry_v[...] = head + jnp.where(
        (row >> shift) == group, (row & (group_len - 1)) * 8192 + LOCAL, slot * 8192
    )
    copies[-1].start()
    for i in range(EARLY, n_chunks):
        fetch(i, 0)
    copies[-1].wait()

    def sort_out(t, n_local):
        entry = entry_s[0, t]
        local_s[n_local] = entry
        remote_s[t - n_local] = entry
        return n_local + (entry >> LOCAL_BIT)

    n_local = lax.fori_loop(0, n_tiles, sort_out, 0, unroll=16)
    n_remote = n_tiles - n_local
    for i in range(PAD):
        local_s[n_local + i] = n_dst * 256 + n_tiles - 1
        remote_s[n_remote + i] = n_dst * 256 + n_tiles - PAD + i
    remote_s[remote_s.shape[0] - 1] = n_remote
    copies[2].wait()
    copies[3].wait()
    copies[4].wait()
    for d in range(n_dst):
        place = pl.multiple_of((ids_s[d] - group * group_len) * 128, 128)
        own = feat_ref[:, pl.ds(place, 128)].astype(jnp.float32)
        acc_ref[d] = coef_ref[d : d + 1, :] * own
    acc_ref[n_dst] = jnp.zeros((8, 128), jnp.float32)
    def load_x(place):
        return feat_ref[:, pl.ds(pl.multiple_of(place * 128, 128), 128)].astype(jnp.float32)

    ready = tile_passes(
        local_s, 0, (n_local + BATCH - 1) // BATCH, load_x, lambda _, tile: adj_ref[tile],
        acc_ref, wait_until, 0,
    )
    lax.fori_loop(ready, n_chunks, wait, 0)

    def hold(i, carry):
        held_ref[i] = adj_ref[remote_s[i] & 255]
        return carry

    lax.fori_loop(0, HELD, hold, 0, unroll=8)


def spread_kernel(src_h, feat_h, out_ref, feat_ref, src_v, sems):
    copy = pltpu.make_async_copy(src_h, src_v, sems.at[0])
    copy.start()
    fetch = pltpu.make_async_copy(feat_h, feat_ref, sems.at[1])
    fetch.start()
    copy.wait()
    out_ref[...] = jnp.broadcast_to(src_v[...][None], out_ref.shape)
    fetch.wait()


def gather_kernel(req_ref, feat_ref, out_ref):
    group = lax.axis_index("grp")
    group_len = feat_ref.shape[1] // 128
    shift = group_len.bit_length() - 1
    req = req_ref[...]
    least = four_least(jnp.where((req >> shift) == group, req & (group_len - 1), BIG))
    lane = lax.broadcasted_iota(jnp.int32, (req.shape[0], 128), 1)
    table = jnp.zeros((req.shape[0], 128), jnp.int32)
    for r, low in enumerate(least):
        table = jnp.where(lane == r, jnp.minimum(low, group_len - 1), table)
    for k in range(req.shape[0]):
        for r in range(NEED):
            place = pl.multiple_of(table[k, r] * 128, 128)
            out_ref[k, r] = feat_ref[:, pl.ds(place, 128)]


def remote_kernel(
    remote_s, recv_ref, acc_in_ref, held_ref, adj_h, out_ref, adj_ref, acc_ref, sems
):
    n_remote = remote_s[remote_s.shape[0] - 1]

    n_passes = (jnp.maximum(n_remote - HELD, 0) + LATE - 1) // LATE

    def fetch_some(i, step):
        for q in range(FETCH):
            place = step * LATE + i * FETCH + q
            pltpu.make_async_copy(
                adj_h.at[remote_s[HELD + place] & 255], adj_ref.at[place], sems.at[step]
            ).start()
        return step

    def fetch_pass(step, carry):
        lax.fori_loop(0, LATE // FETCH, fetch_some, step)
        return carry

    lax.fori_loop(0, n_passes, fetch_pass, 0)
    acc_ref[...] = acc_in_ref[...]

    def load_x(slot):
        return recv_ref[slot].astype(jnp.float32)

    def late_pass(step, carry):
        first = pl.multiple_of(step * LATE, LATE)
        pltpu.make_async_copy(
            adj_h.at[pl.ds(0, LATE)], adj_ref.at[pl.ds(first, LATE)], sems.at[step]
        ).wait()
        tile_pass(
            remote_s, HELD + first, LATE, load_x, lambda index, _: adj_ref[index - HELD], acc_ref
        )
        return carry

    tile_pass(remote_s, 0, HELD, load_x, lambda index, _: held_ref[index], acc_ref)
    lax.fori_loop(0, n_passes, late_pass, 0)
    out_ref[...] = acc_ref[: out_ref.shape[0]].astype(out_ref.dtype)


def per_device(features, adj_tiles, tile_dst, tile_src, dst_ids, self_coef, weight, out_bias):
    n_feat = features.shape[0]
    n_tiles = tile_src.shape[0]
    n_dst = dst_ids.shape[0]
    n_grp = lax.axis_size("grp")
    n_slots = n_grp * NEED
    params = pltpu.CompilerParams(vmem_limit_bytes=16 << 20)
    spread, feat_held = pl.pallas_call(
        spread_kernel,
        name="spread",
        out_shape=(
            pltpu.VMEM((n_grp, 1, n_tiles), jnp.int32),
            pltpu.VMEM(features.shape, features.dtype),
        ),
        in_specs=[HBM, HBM],
        out_specs=(VMEM, VMEM),
        scratch_shapes=[pltpu.VMEM((1, n_tiles), jnp.int32), pltpu.SemaphoreType.DMA((2,))],
        compiler_params=pltpu.CompilerParams(vmem_limit_bytes=4 << 20),
    )(
        pltpu.with_memory_space_constraint(tile_src.reshape(1, n_tiles), pltpu.HBM),
        pltpu.with_memory_space_constraint(features, pltpu.HBM),
    )
    requests = lax.all_to_all(spread, "grp", 0, 0, tiled=True).reshape(n_grp, n_tiles)
    acc, adj_held, remote = pl.pallas_call(
        local_kernel,
        name="local",
        out_shape=(
            pltpu.VMEM((n_dst + 1, n_feat, 128), jnp.float32),
            pltpu.VMEM((HELD,) + adj_tiles.shape[1:], adj_tiles.dtype),
            pltpu.SMEM((n_tiles + PAD + 1,), jnp.int32),
        ),
        in_specs=[HBM] * 6,
        out_specs=(VMEM, VMEM, SMEM),
        scratch_shapes=[
            pltpu.VMEM(features.shape, features.dtype),
            pltpu.VMEM(adj_tiles.shape, adj_tiles.dtype),
            pltpu.VMEM((1, n_tiles), jnp.int32),
            pltpu.VMEM((1, n_tiles), jnp.int32),
            pltpu.SMEM((n_dst,), jnp.int32),
            pltpu.VMEM((n_dst, 128), jnp.float32),
            pltpu.SMEM((n_tiles + PAD,), jnp.int32),
            pltpu.VMEM((1, n_tiles), jnp.int32),
            pltpu.SMEM((1, n_tiles), jnp.int32),
            pltpu.SemaphoreType.DMA((6,)),
            pltpu.SemaphoreType.DMA((n_tiles // CHUNK,)),
        ],
        compiler_params=params,
        cost_estimate=pl.CostEstimate(
            flops=2 * n_tiles * 128 * 128 * 32, bytes_accessed=18 << 20, transcendentals=0
        ),
    )(
        *[
            pltpu.with_memory_space_constraint(a, pltpu.HBM)
            for a in (
                tile_src.reshape(1, n_tiles), tile_dst.reshape(1, n_tiles), dst_ids,
                self_coef.reshape(n_dst, 128), features, adj_tiles,
            )
        ]
    )
    blocks = pl.pallas_call(
        gather_kernel,
        name="gather",
        out_shape=jax.ShapeDtypeStruct((n_grp, NEED, n_feat, 128), features.dtype),
        in_specs=[VMEM, VMEM],
        out_specs=VMEM,
        compiler_params=pltpu.CompilerParams(vmem_limit_bytes=4 << 20),
    )(requests, pltpu.with_memory_space_constraint(feat_held, pltpu.VMEM))
    arrived = lax.all_to_all(blocks, "grp", 0, 0, tiled=True).reshape(n_slots, n_feat, 128)
    aggregated = pl.pallas_call(
        remote_kernel,
        name="remote",
        out_shape=jax.ShapeDtypeStruct((n_dst, n_feat, 128), jnp.bfloat16),
        in_specs=[SMEM, VMEM, VMEM, VMEM, HBM],
        out_specs=VMEM,
        scratch_shapes=[
            pltpu.VMEM((-(-(n_tiles - HELD) // LATE) * LATE,) + adj_tiles.shape[1:], adj_tiles.dtype),
            pltpu.VMEM((n_dst + 1, n_feat, 128), jnp.float32),
            pltpu.SemaphoreType.DMA((-(-(n_tiles - HELD) // LATE),)),
        ],
        compiler_params=params,
    )(
        remote, arrived, pltpu.with_memory_space_constraint(acc, pltpu.VMEM),
        pltpu.with_memory_space_constraint(adj_held, pltpu.VMEM),
        pltpu.with_memory_space_constraint(adj_tiles, pltpu.HBM),
    )
    rows = lax.all_to_all(aggregated, "col", 0, 0, tiled=True).reshape(-1, 128)
    mixed = (
        lax.dot_general(
            rows, weight, (((0,), (0,)), ((), ())), preferred_element_type=jnp.float32
        )
        + out_bias
    )
    return jax.nn.relu(mixed).astype(jnp.bfloat16)


def solution(mesh):
    in_specs = (
        P("col", "grp"),
        P("grp", None, None),
        P("grp"),
        P("grp"),
        P("grp"),
        P("grp"),
        P(),
        P(),
    )
    out_specs = P(("grp", "col"), None)
    return jax.shard_map(
        per_device, mesh=mesh, in_specs=in_specs, out_specs=out_specs, check_vma=False
    )
```
